32 devices in a mesh: groups: 2 (over x), vel: 8 (over z, y), sub: 2 (over core).
Axes of the slice: x: 2, y: 2, z: 4, core: 2. Of those that a mesh axis runs over, the one named last changes fastest.
Arguments:
- dist: float32 [16, 256, 1024], P('sub', 'vel', 'groups'), parts along dimension 2, may hold values from 0 to 6, as said below
- cell_type: int32 [1024], P('groups'), parts along dimension 0, may hold values from 0 to 1, as said below
- groove_mask: int32 [64], P('groups'), parts along dimension 0, may hold values 0 or 1
Outputs:
- dist_next: float32 [16, 256, 1024], P('sub', 'vel', 'groups'), parts along dimension 2
The draws below stay inside these ranges and needn't reach their ends.
There are 2 independent parts, one for each index of `groups`. The reference program is written for one: setup_inputs(seed, part) draws one part's arguments, and reference() takes and returns one part's arrays. A program takes and returns all parts, laid end to end along the dimension named above; each array names one. Nothing has to cross between parts.
Inputs may be any that keep to these rules, and one draw needn't show every extreme that they name: `cell_type`: in each column the solid cells are its lowest ones; a column holds at most a quarter of 16 of them, and every draw has columns with that many and columns with none; grooves repeat along the columns with a period of 4 to 12 columns. `dist`: every entry is positive.
All inputs are finite; a program needn't handle non-finite values.
Results may differ from the reference program's by a relative error of at most 0.0001.
Values sent between devices are 32-bit elements; how exact they have to be, the bound alone decides.
A program may use at most 128 MiB of HBM per device.

```python
import math
import jax
import jax.numpy as jnp
from jax import lax

VN = 16
SY = 16
STEPS = 2
CELLS = 512
SX = 32


def draw_cell_type(key, part):
    columns = CELLS // SY
    keys = jax.random.split(jax.random.fold_in(key, 11), 4)
    period = jax.random.randint(keys[0], (), 4, 13)
    width = jax.random.randint(keys[1], (), 1, period)
    phase = jax.random.randint(keys[2], (), 0, period)
    deepest = max(1, SY // 4)
    column = jnp.arange(columns, dtype=jnp.int32)
    offset = (column + phase) % period
    depth = jax.random.randint(keys[3], (columns,), 1, deepest + 1)
    depth = jnp.where(offset == width, deepest, depth)
    depth = jnp.where(offset < width, 0, depth)
    height = jnp.arange(CELLS, dtype=jnp.int32) % SY
    return (height < jnp.repeat(depth, SY)).astype(jnp.int32)


def draw_dist(key, part):
    spacing = 10.0 / VN
    index = jnp.arange(VN, dtype=jnp.float32)
    speed = (index - (VN - 1) / 2.0) * spacing
    keys = jax.random.split(jax.random.fold_in(key, 7), 7)
    density = jnp.exp(jax.random.uniform(keys[0], (CELLS,), minval=-0.7, maxval=0.7))
    rough = 1.0 + 0.2 * jax.random.truncated_normal(keys[3], -2.5, 2.5, (VN, VN, VN, CELLS))
    second_rough = jax.random.uniform(keys[5], (VN, VN, VN, CELLS), minval=0.3, maxval=1.7)
    drift = jax.random.uniform(keys[1], (CELLS,), minval=-2.0, maxval=2.0)
    heat = jax.random.uniform(keys[2], (CELLS,), minval=0.7, maxval=2.5)
    level = jax.random.uniform(keys[4], (CELLS,), minval=0.1, maxval=0.25)
    holes = jax.random.bernoulli(keys[6], 0.03, (VN, VN, VN, CELLS))
    factor = jnp.where(holes, 0.0001, 1.0)
    speed_y = speed[:, None, None, None]
    speed_x = speed[None, :, None, None]
    speed_z = speed[None, None, :, None]
    square = (speed_x - drift) * (speed_x - drift) + speed_y * speed_y + speed_z * speed_z
    values = density * (jnp.exp(-square / (2.0 * heat)) * rough + level * second_rough) * factor
    return values.reshape(VN, VN * VN, CELLS).astype(jnp.float32)


def touch_ends(array, stream_key, least, top_value):
    longest = array.shape.index(max(array.shape))
    spots = []
    for shift in (0, 1):
        where = [jax.random.randint(jax.random.fold_in(stream_key, axis), (), 0, length) for axis, length in enumerate(array.shape)]
        where[longest] = (where[longest] + shift) % array.shape[longest]
        spots.append(tuple(where))
    return array.at[spots[0]].set(least).at[spots[1]].set(top_value)


def setup_inputs(seed: int = 0, part: int = 0) -> dict:
    arg_keys = jax.random.split(jax.random.key(seed), 4)
    part_keys = jax.random.split(jax.random.fold_in(arg_keys[3], part), 4)
    dist = draw_dist(jax.random.fold_in(jax.random.fold_in(arg_keys[3], part), 71), part)
    cell_type = draw_cell_type(jax.random.fold_in(jax.random.fold_in(arg_keys[3], part), 71), part)
    groove_mask = touch_ends((jax.random.randint(part_keys[2], (SX,), 0, 2) < 1).astype(jnp.int32), jax.random.fold_in(part_keys[2], 1), 0, 1)
    return {"dist": dist, "cell_type": cell_type, "groove_mask": groove_mask}


VEL_RANGE = 5.0
TOP_SPEED = 1.0
ACC_LAND = 0.4
ACC_TOP = 0.7
KNUDSEN = 1.0
HIGHEST = lax.Precision.HIGHEST


def spacing_of(count):
    return 2.0 * VEL_RANGE / count


def time_step(count):
    return 0.8 / ((count - 1) * spacing_of(count))


def speeds(index, count):
    return (index.astype(jnp.float32) - (count - 1) / 2.0) * spacing_of(count)


def wave_numbers(count):
    index = jnp.arange(count, dtype=jnp.int32)
    wrapped = jnp.where(index < count // 2, index, index - count)
    return wrapped.astype(jnp.float32) * (math.pi / VEL_RANGE)


def kernels(count):
    wave = wave_numbers(count)
    wave_y = wave[:, None, None]
    wave_x = wave[None, :, None]
    wave_z = wave[None, None, :]
    square = wave_y * wave_y + wave_x * wave_x + wave_z * wave_z
    first = 1.0 / (1.0 + square / 12.0)
    second = 3.0 * jnp.cos(0.9 * wave_x) / (1.0 + square / 10.0)
    damped = 1.0 + square / 9.0
    loss = 3.0 / (damped * damped)
    return first, second, loss


def full_grid(count):
    index = jnp.arange(count * count * count, dtype=jnp.int32)
    velocity_y = speeds(index // (count * count), count)
    velocity_x = speeds((index // count) % count, count)
    velocity_z = speeds(index % count, count)
    return velocity_x, velocity_y, velocity_z


def wall_tables(velocity_x, velocity_y, velocity_z):
    rest = jnp.exp(-(velocity_x * velocity_x + velocity_y * velocity_y + velocity_z * velocity_z) / 2.0)
    shifted = velocity_x - TOP_SPEED
    moving = jnp.exp(-(shifted * shifted + velocity_y * velocity_y + velocity_z * velocity_z) / 2.0)
    weights = jnp.stack([jnp.maximum(-velocity_x, 0.0), jnp.maximum(velocity_x, 0.0), jnp.maximum(-velocity_y, 0.0), jnp.maximum(velocity_y, 0.0)])
    return rest, moving, weights


def wall_norms(count):
    velocity_x, velocity_y, velocity_z = full_grid(count)
    rest, moving, weights = wall_tables(velocity_x, velocity_y, velocity_z)
    return (jnp.sum(jnp.maximum(velocity_x, 0.0) * rest), jnp.sum(jnp.maximum(-velocity_x, 0.0) * rest), jnp.sum(jnp.maximum(velocity_y, 0.0) * rest), jnp.sum(jnp.maximum(-velocity_y, 0.0) * moving))


def cell_masks(cell_type, groove_mask, height_count):
    total = cell_type.shape[0]
    solid = cell_type.astype(jnp.float32)
    height = jnp.arange(total, dtype=jnp.int32) % height_count
    left_solid = jnp.roll(solid, height_count)
    right_solid = jnp.roll(solid, -height_count)
    below_solid = jnp.where(height == 0, 1.0, jnp.roll(solid, 1))
    top_wall = jnp.where(height == height_count - 1, 1.0, 0.0 * solid)
    accommodation = jnp.repeat(jnp.where(groove_mask == 1, 1.0, ACC_LAND), height_count)
    return jnp.stack([left_solid, right_solid, below_solid, top_wall, accommodation, 1.0 - solid])


def advance(center, left, right, below, above, mirror, flux, masks, velocity, norms, step_size):
    velocity_x, velocity_y, rest, moving = velocity
    left_solid = masks[0][None, :]
    right_solid = masks[1][None, :]
    below_solid = masks[2][None, :]
    top_wall = masks[3][None, :]
    accommodation = masks[4][None, :]
    fluid = masks[5][None, :]
    left_ghost = (flux[0] / norms[0])[None, :] * rest
    right_ghost = (flux[1] / norms[1])[None, :] * rest
    below_ghost = (1.0 - accommodation) * mirror + accommodation * (flux[2] / norms[2])[None, :] * rest
    above_ghost = (1.0 - ACC_TOP) * mirror + ACC_TOP * (flux[3] / norms[3])[None, :] * moving
    left_value = jnp.where(left_solid > 0.0, left_ghost, left)
    right_value = jnp.where(right_solid > 0.0, right_ghost, right)
    below_value = jnp.where(below_solid > 0.0, below_ghost, below)
    above_value = jnp.where(top_wall > 0.0, above_ghost, above)
    change = jnp.maximum(velocity_x, 0.0) * (center - left_value) + jnp.minimum(velocity_x, 0.0) * (right_value - center)
    change = change + jnp.maximum(velocity_y, 0.0) * (center - below_value) + jnp.minimum(velocity_y, 0.0) * (above_value - center)
    return (center - step_size * change) * fluid


def collide_exact(cube, tables, rate):
    spectrum = jnp.fft.fftn(cube, axes=(0, 1, 2))

    def inverse(table):
        return jnp.real(jnp.fft.ifftn(table[..., None] * spectrum, axes=(0, 1, 2)))

    gain = inverse(tables[0]) * inverse(tables[1])
    return cube + rate * (gain - cube * inverse(tables[2]))


def reference(dist, cell_type, groove_mask):
    count = VN
    height_count = SY
    total_cells = dist.shape[2]
    volume = count * count * count
    masks = cell_masks(cell_type, groove_mask, height_count)
    norms = wall_norms(count)
    step_size = time_step(count)
    rate = step_size / KNUDSEN
    tables = kernels(count)
    grid_x, grid_y, grid_z = full_grid(count)
    rest, moving, weights = wall_tables(grid_x, grid_y, grid_z)
    velocity = (grid_x[:, None], grid_y[:, None], rest[:, None], moving[:, None])
    block = math.gcd(total_cells, 512)
    state = dist.reshape(volume, total_cells)
    for iteration in range(STEPS):
        blocks = jnp.moveaxis(state.reshape(count, count, count, total_cells // block, block), 3, 0)
        post = lax.map(lambda piece: collide_exact(piece, tables, rate), blocks)
        post = jnp.moveaxis(post, 0, 3).reshape(volume, total_cells)
        flux = jnp.dot(weights, post, precision=HIGHEST)
        mirror = post.reshape(count, count * count, total_cells)[::-1].reshape(volume, total_cells)
        state = advance(post, jnp.roll(post, height_count, 1), jnp.roll(post, -height_count, 1), jnp.roll(post, 1, 1), jnp.roll(post, -1, 1), mirror, flux, masks, velocity, norms, step_size)
    return state.reshape(count, count * count, total_cells)
```

```python
import functools
import math

import jax
import jax.numpy as jnp
import numpy as np
from jax import lax
from jax.experimental import pallas as pl
from jax.experimental.pallas import tpu as pltpu
from jax.sharding import PartitionSpec as P

VN = 16
SY = 16
STEPS = 2

VEL_RANGE = 5.0
TOP_SPEED = 1.0
ACC_LAND = 0.4
ACC_TOP = 0.7
KNUDSEN = 1.0
HALF = VN // 2
PLANE = VN * VN
LANES = 128
CHUNK = 32
MESH = pl.DeviceIdType.MESH
F32 = jnp.float32
BF16 = jnp.bfloat16


def real_basis():
    place = np.arange(VN) - (VN - 1) / 2.0
    modes = np.concatenate([np.arange(HALF), np.arange(1, HALF + 1)])
    rows = []
    for index, mode in enumerate(modes):
        angle = 2.0 * math.pi * mode * place / VN
        row = np.cos(angle) if index < HALF else np.sin(angle)
        rows.append(row / np.sqrt(np.sum(row * row)))
    return modes, np.stack(rows)


def halves(table):
    high = table.astype(np.float32).astype(jnp.bfloat16)
    low = (table - high.astype(np.float64)).astype(jnp.bfloat16)
    return high, low


def left_table(table):
    high, low = halves(table)
    return np.concatenate([high, high, low], axis=1)


def right_table(table):
    high, low = halves(table)
    return np.concatenate([high, high, low], axis=0)


@functools.cache
def constants():
    modes, basis = real_basis()
    step = 2.0 * VEL_RANGE / VN
    plane = np.kron(basis, basis)
    same = np.eye(CHUNK)
    forward = left_table(plane)
    inverse = left_table(plane.T)
    even = np.kron(basis[:HALF, :HALF].T, same)
    odd = np.kron(basis[HALF:, :HALF].T, same)
    height = np.stack([right_table(t) for t in (even, odd, even.T, odd.T)])
    wave = modes * (math.pi / VEL_RANGE)
    along_y = wave[:, None, None]
    along_x = wave[None, :, None]
    along_z = wave[None, None, :]
    square = along_y**2 + along_x**2 + along_z**2
    first = 1.0 / (1.0 + square / 12.0)
    second = 3.0 * np.cos(0.9 * along_x) / (1.0 + square / 10.0)
    loss = 3.0 / (1.0 + square / 9.0) ** 2
    tables = []
    for table in (first, second, loss):
        table = table.reshape(2, HALF, PLANE).transpose(0, 2, 1)
        tables.append(np.repeat(table, CHUNK, axis=2))
    tables = np.stack(tables).astype(np.float32)

    speed = (np.arange(VN) - (VN - 1) / 2.0) * step
    dt = 0.8 / ((VN - 1) * step)
    gauss = np.exp(-speed * speed / 2.0)
    moving = np.exp(-((speed - TOP_SPEED) ** 2) / 2.0)
    speed_x = np.repeat(speed, VN)
    rows = np.stack([np.abs(speed_x), np.kron(gauss, gauss), np.kron(moving, gauss)])
    rows = np.broadcast_to(rows[:, :, None], (3, PLANE, LANES)).astype(np.float32)
    lanes = np.zeros((8, LANES))
    for part in range(2):
        lanes[part] = np.repeat(np.abs(speed[4 * part : 4 * part + 4]), CHUNK)
        lanes[2 + part] = np.repeat(gauss[4 * part : 4 * part + 4], CHUNK)
    up = np.sum(np.maximum(speed, 0.0) * gauss)
    total = np.sum(gauss)
    norms = (
        up * total * total,
        up * total * total,
        up * total * total,
        up * np.sum(moving) * total,
    )
    return forward, inverse, height, tables, rows, lanes.astype(np.float32), dt, norms


def roll(value, shift):
    return pltpu.roll(value, shift % LANES, 1)


def chunk_transpose(parts, low_pair, even_chunk):
    a0, a1, a2, a3 = parts
    b0 = jnp.where(low_pair, a0, roll(a2, 64))
    b2 = jnp.where(low_pair, roll(a0, 64), a2)
    b1 = jnp.where(low_pair, a1, roll(a3, 64))
    b3 = jnp.where(low_pair, roll(a1, 64), a3)
    return (
        jnp.where(even_chunk, b0, roll(b1, 32)),
        jnp.where(even_chunk, roll(b0, -32), b1),
        jnp.where(even_chunk, b2, roll(b3, 32)),
        jnp.where(even_chunk, roll(b2, -32), b3),
    )


def split(value):
    high = value.astype(BF16)
    low = (value - high.astype(F32)).astype(BF16)
    return high, low


def kernel(
    vel_count, dt, norms,
    cell_ref, groove_ref, dist_ref, forward_hbm, inverse_hbm, height_hbm, tables_hbm, rows_hbm,
    lanes_ref, out_ref,
    stage, back, grid, post, gains, halo_out, halo_in, forward, inverse, height, tables, rows,
    table_sem, own_sem, send_sem, recv_sem, halo_send, halo_recv, back_send, back_recv,
):
    devices = 2 * vel_count
    depth = dist_ref.shape[1]
    group = lax.axis_index("groups")
    vel = lax.axis_index("vel")
    sub = lax.axis_index("sub")
    ring = vel // 2 + (vel % 2) * (vel_count - 1 - 2 * (vel // 2))
    me = 2 * ring + sub

    def place_of(position):
        index = position // 2
        far = index // (vel_count // 2)
        return 2 * index + far * (2 * (vel_count - 1 - index) + 1 - 2 * index), position % 2

    def device_of(position):
        v, s = place_of(position)
        return (group, v, s)

    loads = [
        pltpu.make_async_copy(source, target, table_sem.at[index])
        for index, (source, target) in enumerate(
            (
                (forward_hbm, forward),
                (inverse_hbm, inverse),
                (height_hbm, height),
                (tables_hbm, tables),
                (rows_hbm, rows),
            )
        )
    ]
    for load in loads:
        load.start()

    barrier = pltpu.get_barrier_semaphore()

    @pl.loop(1, devices)
    def _(offset):
        pl.semaphore_signal(
            barrier, inc=1, device_id=device_of((me + offset) % devices), device_id_type=MESH
        )

    pl.semaphore_wait(barrier, devices - 1)

    lane = lax.broadcasted_iota(jnp.int32, (1, LANES), 1)
    low_pair = lane < 64
    even_chunk = lane % 64 < 32
    first_column = lane % CHUNK < SY
    level = lane % SY

    def outward(position):
        return pltpu.make_async_remote_copy(
            src_ref=stage.at[position],
            dst_ref=grid.at[pl.ds(2 * sub, 2), pl.ds(vel * depth, depth), :],
            send_sem=send_sem.at[position],
            recv_sem=recv_sem.at[me],
            device_id=device_of(position),
            device_id_type=MESH,
        )

    @pl.loop(0, devices // 4)
    def _(turn):
        block = (turn + me // 4) % (devices // 4)
        start = pl.multiple_of(block * LANES, LANES)
        for part in range(2):
            pieces = []
            for index in range(4):
                m = 4 * part + index
                y = m + sub * (HALF - 1 - 2 * m)
                pieces.append(dist_ref[y, :, pl.ds(start, LANES)])
            for index, piece in enumerate(chunk_transpose(pieces, low_pair, even_chunk)):
                stage[4 * block + index, part] = piece
        for index in range(4):
            position = 4 * block + index

            @pl.when(position != me)
            def _():
                outward(position).start()

    own = pltpu.make_async_copy(
        stage.at[me], grid.at[pl.ds(2 * sub, 2), pl.ds(vel * depth, depth), :], own_sem.at[0]
    )
    own.start()

    cells = CHUNK * devices

    def solid_count(column):
        count = jnp.int32(0)
        for index in range(SY):
            count = count + cell_ref[column * SY + index]
        return count

    columns = cells // SY
    count_first = solid_count(2 * me)
    count_second = solid_count(2 * me + 1)
    count_left = solid_count((2 * me + columns - 1) % columns)
    count_right = solid_count((2 * me + 2) % columns)
    count = jnp.where(first_column, count_first, count_second)
    left_solid = level < jnp.where(first_column, count_left, count_first)
    right_solid = level < jnp.where(first_column, count_second, count_right)
    below_solid = level <= count
    top_wall = level == SY - 1
    fluid = jnp.where(level < count, 0.0, 1.0)
    groove = jnp.where(first_column, groove_ref[2 * me], groove_ref[2 * me + 1])
    accommodation = jnp.where(groove == 1, 1.0, ACC_LAND)

    for load in loads:
        load.wait()
    own.wait()

    @pl.loop(1, devices)
    def _(offset):
        source = (me + devices - offset) % devices
        v, s = place_of(source)
        pltpu.make_async_remote_copy(
            src_ref=stage.at[source],
            dst_ref=grid.at[pl.ds(2 * s, 2), pl.ds(v * depth, depth), :],
            send_sem=send_sem.at[source],
            recv_sem=recv_sem.at[source],
            device_id=device_of(source),
            device_id_type=MESH,
        ).wait_recv()

    rate = dt / KNUDSEN
    right_device = device_of((me + 1) % devices)
    left_device = device_of((me + devices - 1) % devices)

    def by_height(value, index):
        high, low = split(value)
        return jnp.dot(
            jnp.concatenate([high, low, high], axis=1), height[index], preferred_element_type=F32
        )

    def by_plane(table, value):
        high, low = split(value)
        return jnp.dot(
            table[...], jnp.concatenate([high, low, high], axis=0), preferred_element_type=F32
        )

    @pl.loop(0, STEPS)
    def _(step):
        for parity in range(2):
            if parity == 0:
                folded = [grid[0] + grid[2], grid[1] + grid[3]]
            else:
                folded = [grid[0] - grid[2], grid[1] - grid[3]]
            spectrum = by_plane(forward, by_height(jnp.concatenate(folded, axis=1), parity))
            for index in range(3):
                gains[index, parity] = by_height(
                    by_plane(inverse, spectrum * tables[index, parity]), 2 + parity
                )

        def collided(q, low, high):
            part = q % 2
            lanes = slice(LANES * part, LANES * part + LANES)
            found = []
            for index in range(3):
                even = gains[index, 0, low:high, lanes]
                odd = gains[index, 1, low:high, lanes]
                found.append(even + odd if q < 2 else even - odd)
            value = grid[q, low:high]
            return value + rate * (found[0] * found[1] - value * found[2])

        flux_x = [jnp.zeros((1, LANES), F32), jnp.zeros((1, LANES), F32)]
        flux_y = [jnp.zeros((1, LANES), F32), jnp.zeros((1, LANES), F32)]
        copies = []
        for side in range(2):
            low, high = side * (PLANE // 2), (side + 1) * (PLANE // 2)
            for pair in range(2):
                values = []
                for part in range(2):
                    q = 2 * pair + part
                    value = collided(q, low, high)
                    post[q, low:high] = value
                    values.append(value)
                    flux_x[side] = flux_x[side] + jnp.sum(
                        value * rows[0, low:high], axis=0, keepdims=True
                    )
                    flux_y[pair] = flux_y[pair] + lanes_ref[part : part + 1] * jnp.sum(
                        value, axis=0, keepdims=True
                    )
                if side == 0:
                    packed = jnp.where(first_column, values[1], roll(values[0], SY))
                else:
                    packed = jnp.where(first_column, roll(values[0], -SY), values[1])
                halo_out[2 * step + side, pair] = packed
            copy = pltpu.make_async_remote_copy(
                src_ref=halo_out.at[2 * step + side],
                dst_ref=halo_in.at[2 * step + side],
                send_sem=halo_send.at[2 * step + side],
                recv_sem=halo_recv.at[2 * step + side],
                device_id=left_device if side == 0 else right_device,
                device_id_type=MESH,
            )
            copy.start()
            copies.append(copy)

        def over_chunks(value):
            value = value + roll(value, 64)
            return value + roll(value, 32)

        flux = [over_chunks(f) for f in flux_x + flux_y]
        for side in range(2):
            low, high = side * (PLANE // 2), (side + 1) * (PLANE // 2)
            copies[side].wait()
            for pair in range(2):
                packed = halo_in[2 * step + side, pair]
                for part in range(2):
                    q = 2 * pair + part
                    center = post[q, low:high]
                    mirror = post[2 * (1 - pair) + part, low:high]
                    gauss_y = lanes_ref[2 + part : 3 + part]
                    if side == 0:
                        edge = packed if part == 0 else roll(packed, SY)
                        across = jnp.where(first_column, roll(center, -SY), edge)
                        solid = right_solid
                        scale = flux[1] / norms[1]
                    else:
                        edge = packed if part == 0 else roll(packed, -SY)
                        across = jnp.where(first_column, edge, roll(center, SY))
                        solid = left_solid
                        scale = flux[0] / norms[0]
                    rest = rows[1, low:high]
                    across = jnp.where(solid, rest * (scale * gauss_y), across)
                    if pair == 0:
                        ghost = (1.0 - ACC_TOP) * mirror + rows[2, low:high] * (
                            flux[3] * (gauss_y * (ACC_TOP / norms[3]))
                        )
                        along = jnp.where(top_wall, ghost, roll(center, -1))
                    else:
                        ghost = (1.0 - accommodation) * mirror + rest * (
                            accommodation * flux[2] * (gauss_y / norms[2])
                        )
                        along = jnp.where(below_solid, ghost, roll(center, 1))
                    change = rows[0, low:high] * (center - across) + lanes_ref[
                        part : part + 1
                    ] * (center - along)
                    grid[q, low:high] = (center - dt * change) * fluid

    def homeward(position):
        v, s = place_of(position)
        return pltpu.make_async_remote_copy(
            src_ref=grid.at[pl.ds(2 * s, 2), pl.ds(v * depth, depth), :],
            dst_ref=back.at[me],
            send_sem=back_send.at[position],
            recv_sem=back_recv.at[me],
            device_id=device_of(position),
            device_id_type=MESH,
        )

    @pl.loop(1, devices)
    def _(offset):
        homeward((me + offset) % devices).start()

    own_back = pltpu.make_async_copy(
        grid.at[pl.ds(2 * sub, 2), pl.ds(vel * depth, depth), :], back.at[me], own_sem.at[1]
    )
    own_back.start()

    @pl.loop(1, devices)
    def _(offset):
        outward((me + offset) % devices).wait_send()

    own_back.wait()

    @pl.loop(1, devices)
    def _(offset):
        source = (me + devices - offset) % devices
        pltpu.make_async_remote_copy(
            src_ref=stage.at[source],
            dst_ref=back.at[source],
            send_sem=back_send.at[source],
            recv_sem=back_recv.at[source],
            device_id=device_of(source),
            device_id_type=MESH,
        ).wait_recv()

    @pl.loop(0, devices // 4)
    def _(block):
        start = pl.multiple_of(block * LANES, LANES)
        for part in range(2):
            pieces = [back[4 * block + index, part] for index in range(4)]
            for index, piece in enumerate(chunk_transpose(pieces, low_pair, even_chunk)):
                m = 4 * part + index
                y = m + sub * (HALF - 1 - 2 * m)
                out_ref[y, :, pl.ds(start, LANES)] = piece

    @pl.loop(1, devices)
    def _(offset):
        homeward((me + offset) % devices).wait_send()


def solution(mesh):
    vel_count = mesh.shape["vel"]
    devices = 2 * vel_count
    forward, inverse, height, tables, rows, lanes, dt, norms = constants()
    depth = PLANE // vel_count

    def local(dist, cell_type, groove_mask):
        hbm = pl.BlockSpec(memory_space=pl.ANY)
        vmem = pl.BlockSpec(memory_space=pltpu.VMEM)
        smem = pl.BlockSpec(memory_space=pltpu.SMEM)
        dma = pltpu.SemaphoreType.DMA
        piece = (2, depth, LANES)
        return pl.pallas_call(
            functools.partial(kernel, vel_count, dt, norms),
            out_shape=jax.ShapeDtypeStruct(dist.shape, F32),
            in_specs=[smem, smem, vmem, hbm, hbm, hbm, hbm, hbm, vmem],
            out_specs=vmem,
            scratch_shapes=[
                pltpu.VMEM((devices,) + piece, F32),
                pltpu.VMEM((devices,) + piece, F32),
                pltpu.VMEM((4, PLANE, LANES), F32),
                pltpu.VMEM((4, PLANE, LANES), F32),
                pltpu.VMEM((3, 2, PLANE, PLANE), F32),
                pltpu.VMEM((2 * STEPS, 2, PLANE // 2, LANES), F32),
                pltpu.VMEM((2 * STEPS, 2, PLANE // 2, LANES), F32),
                pltpu.VMEM(forward.shape, BF16),
                pltpu.VMEM(inverse.shape, BF16),
                pltpu.VMEM(height.shape, BF16),
                pltpu.VMEM(tables.shape, F32),
                pltpu.VMEM(rows.shape, F32),
                dma((5,)),
                dma((2,)),
                dma((devices,)),
                dma((devices,)),
                dma((2 * STEPS,)),
                dma((2 * STEPS,)),
                dma((devices,)),
                dma((devices,)),
            ],
            compiler_params=pltpu.CompilerParams(
                collective_id=0, has_side_effects=True, vmem_limit_bytes=40 * 1024 * 1024
            ),
        )(
            cell_type, groove_mask, dist,
            jnp.asarray(forward), jnp.asarray(inverse), jnp.asarray(height),
            jnp.asarray(tables), jnp.asarray(rows), jnp.asarray(lanes),
        )

    return jax.shard_map(
        local,
        mesh=mesh,
        in_specs=(P("sub", "vel", "groups"), P("groups"), P("groups")),
        out_specs=P("sub", "vel", "groups"),
        check_vma=False,
    )
```

```python
import functools
import math

import jax
import jax.numpy as jnp
import numpy as np
from jax import lax
from jax.experimental import pallas as pl
from jax.experimental.pallas import tpu as pltpu
from jax.sharding import PartitionSpec as P

VN = 16
SY = 16
STEPS = 2

VEL_RANGE = 5.0
TOP_SPEED = 1.0
ACC_LAND = 0.4
ACC_TOP = 0.7
KNUDSEN = 1.0
HALF = VN // 2
PLANE = VN * VN
LANES = 128
CHUNK = 32
MESH = pl.DeviceIdType.MESH
F32 = jnp.float32
BF16 = jnp.bfloat16


def real_basis():
    place = np.arange(VN) - (VN - 1) / 2.0
    modes = np.concatenate([np.arange(HALF), np.arange(1, HALF + 1)])
    rows = []
    for index, mode in enumerate(modes):
        angle = 2.0 * math.pi * mode * place / VN
        row = np.cos(angle) if index < HALF else np.sin(angle)
        rows.append(row / np.sqrt(np.sum(row * row)))
    return modes, np.stack(rows)


def halves(table):
    high = table.astype(np.float32).astype(jnp.bfloat16)
    low = (table - high.astype(np.float64)).astype(jnp.bfloat16)
    return high, low


def left_table(table):
    high, low = halves(table)
    return np.concatenate([high, high, low], axis=1)


def right_table(table):
    high, low = halves(table)
    return np.concatenate([high, high, low], axis=0)


@functools.cache
def constants():
    modes, basis = real_basis()
    step = 2.0 * VEL_RANGE / VN
    plane = np.kron(basis, basis)
    same = np.eye(CHUNK)
    forward = left_table(plane)
    inverse = left_table(plane.T)
    even = np.kron(basis[:HALF, :HALF].T, same)
    odd = np.kron(basis[HALF:, :HALF].T, same)
    height = np.stack([right_table(t) for t in (even, odd, even.T, odd.T)])
    wave = modes * (math.pi / VEL_RANGE)
    along_y = wave[:, None, None]
    along_x = wave[None, :, None]
    along_z = wave[None, None, :]
    square = along_y**2 + along_x**2 + along_z**2
    first = 1.0 / (1.0 + square / 12.0)
    second = 3.0 * np.cos(0.9 * along_x) / (1.0 + square / 10.0)
    loss = 3.0 / (1.0 + square / 9.0) ** 2
    tables = []
    for table in (first, second, loss):
        table = table.reshape(2, HALF, PLANE).transpose(0, 2, 1)
        tables.append(np.repeat(table, CHUNK, axis=2))
    tables = np.stack(tables).astype(np.float32)

    speed = (np.arange(VN) - (VN - 1) / 2.0) * step
    dt = 0.8 / ((VN - 1) * step)
    gauss = np.exp(-speed * speed / 2.0)
    moving = np.exp(-((speed - TOP_SPEED) ** 2) / 2.0)
    speed_x = np.repeat(speed, VN)
    rows = np.stack([np.abs(speed_x), np.kron(gauss, gauss), np.kron(moving, gauss)])
    rows = np.broadcast_to(rows[:, :, None], (3, PLANE, LANES)).astype(np.float32)
    lanes = np.zeros((8, LANES))
    for part in range(2):
        lanes[part] = np.repeat(np.abs(speed[4 * part : 4 * part + 4]), CHUNK)
        lanes[2 + part] = np.repeat(gauss[4 * part : 4 * part + 4], CHUNK)
    up = np.sum(np.maximum(speed, 0.0) * gauss)
    total = np.sum(gauss)
    norms = (
        up * total * total,
        up * total * total,
        up * total * total,
        up * np.sum(moving) * total,
    )
    return forward, inverse, height, tables, rows, lanes.astype(np.float32), dt, norms


def roll(value, shift):
    return pltpu.roll(value, shift % LANES, 1)


def chunk_transpose(parts, low_pair, even_chunk):
    a0, a1, a2, a3 = parts
    b0 = jnp.where(low_pair, a0, roll(a2, 64))
    b2 = jnp.where(low_pair, roll(a0, 64), a2)
    b1 = jnp.where(low_pair, a1, roll(a3, 64))
    b3 = jnp.where(low_pair, roll(a1, 64), a3)
    return (
        jnp.where(even_chunk, b0, roll(b1, 32)),
        jnp.where(even_chunk, roll(b0, -32), b1),
        jnp.where(even_chunk, b2, roll(b3, 32)),
        jnp.where(even_chunk, roll(b2, -32), b3),
    )


def split(value):
    high = value.astype(BF16)
    low = (value - high.astype(F32)).astype(BF16)
    return high, low


def kernel(
    vel_count, dt, norms,
    cell_ref, groove_ref, dist_hbm, forward_hbm, inverse_hbm, height_hbm, tables_hbm, rows_hbm,
    lanes_ref, out_ref,
    dist_ref, stage, back, grid, post, gains, halo_out, halo_in, forward, inverse, height, tables, rows,
    table_sem, own_sem, send_sem, recv_sem, halo_send, halo_recv, back_send, back_recv,
):
    devices = 2 * vel_count
    depth = dist_ref.shape[1]
    fetch = pltpu.make_async_copy(dist_hbm, dist_ref, own_sem.at[2])
    fetch.start()
    group = lax.axis_index("groups")
    vel = lax.axis_index("vel")
    sub = lax.axis_index("sub")
    ring = vel // 2 + (vel % 2) * (vel_count - 1 - 2 * (vel // 2))
    me = 2 * ring + sub

    def place_of(position):
        index = position // 2
        far = index // (vel_count // 2)
        return 2 * index + far * (2 * (vel_count - 1 - index) + 1 - 2 * index), position % 2

    def device_of(position):
        v, s = place_of(position)
        return (group, v, s)

    loads = [
        pltpu.make_async_copy(source, target, table_sem.at[index])
        for index, (source, target) in enumerate(
            (
                (forward_hbm, forward),
                (inverse_hbm, inverse),
                (height_hbm, height),
                (tables_hbm, tables),
                (rows_hbm, rows),
            )
        )
    ]
    for load in loads:
        load.start()

    barrier = pltpu.get_barrier_semaphore()

    @pl.loop(1, devices)
    def _(offset):
        pl.semaphore_signal(
            barrier, inc=1, device_id=device_of((me + offset) % devices), device_id_type=MESH
        )

    pl.semaphore_wait(barrier, devices - 1)
    fetch.wait()

    lane = lax.broadcasted_iota(jnp.int32, (1, LANES), 1)
    low_pair = lane < 64
    even_chunk = lane % 64 < 32
    first_column = lane % CHUNK < SY
    level = lane % SY

    blocks = devices // 4
    mine = me // 4

    def far_first(turn):
        ahead = 1 - 2 * (mine % 2)
        return (mine + ahead * (1 + turn) + 2 * blocks) % blocks

    def outward(position):
        return pltpu.make_async_remote_copy(
            src_ref=stage.at[position],
            dst_ref=grid.at[pl.ds(2 * sub, 2), pl.ds(vel * depth, depth), :],
            send_sem=send_sem.at[position],
            recv_sem=recv_sem.at[me],
            device_id=device_of(position),
            device_id_type=MESH,
        )

    @pl.loop(0, devices // 4)
    def _(turn):
        block = far_first(turn)
        start = pl.multiple_of(block * LANES, LANES)
        for part in range(2):
            pieces = []
            for index in range(4):
                m = 4 * part + index
                y = m + sub * (HALF - 1 - 2 * m)
                pieces.append(dist_ref[y, :, pl.ds(start, LANES)])
            for index, piece in enumerate(chunk_transpose(pieces, low_pair, even_chunk)):
                stage[4 * block + index, part] = piece
        for index in range(4):
            position = 4 * block + index

            @pl.when(position != me)
            def _():
                outward(position).start()

    own = pltpu.make_async_copy(
        stage.at[me], grid.at[pl.ds(2 * sub, 2), pl.ds(vel * depth, depth), :], own_sem.at[0]
    )
    own.start()

    cells = CHUNK * devices

    def solid_count(column):
        count = jnp.int32(0)
        for index in range(SY):
            count = count + cell_ref[column * SY + index]
        return count

    columns = cells // SY
    count_first = solid_count(2 * me)
    count_second = solid_count(2 * me + 1)
    count_left = solid_count((2 * me + columns - 1) % columns)
    count_right = solid_count((2 * me + 2) % columns)
    count = jnp.where(first_column, count_first, count_second)
    left_solid = level < jnp.where(first_column, count_left, count_first)
    right_solid = level < jnp.where(first_column, count_second, count_right)
    below_solid = level <= count
    top_wall = level == SY - 1
    fluid = jnp.where(level < count, 0.0, 1.0)
    groove = jnp.where(first_column, groove_ref[2 * me], groove_ref[2 * me + 1])
    accommodation = jnp.where(groove == 1, 1.0, ACC_LAND)

    for load in loads:
        load.wait()
    own.wait()

    @pl.loop(1, devices)
    def _(offset):
        source = (me + devices - offset) % devices
        v, s = place_of(source)
        pltpu.make_async_remote_copy(
            src_ref=stage.at[source],
            dst_ref=grid.at[pl.ds(2 * s, 2), pl.ds(v * depth, depth), :],
            send_sem=send_sem.at[source],
            recv_sem=recv_sem.at[source],
            device_id=device_of(source),
            device_id_type=MESH,
        ).wait_recv()

    rate = dt / KNUDSEN
    right_device = device_of((me + 1) % devices)
    left_device = device_of((me + devices - 1) % devices)

    def by_height(value, index):
        high, low = split(value)
        return jnp.dot(
            jnp.concatenate([high, low, high], axis=1), height[index], preferred_element_type=F32
        )

    def by_plane(table, value):
        high, low = split(value)
        return jnp.dot(
            table[...], jnp.concatenate([high, low, high], axis=0), preferred_element_type=F32
        )

    @pl.loop(0, STEPS)
    def _(step):
        for parity in range(2):
            if parity == 0:
                folded = [grid[0] + grid[2], grid[1] + grid[3]]
            else:
                folded = [grid[0] - grid[2], grid[1] - grid[3]]
            spectrum = by_plane(forward, by_height(jnp.concatenate(folded, axis=1), parity))
            for index in range(3):
                gains[index, parity] = by_height(
                    by_plane(inverse, spectrum * tables[index, parity]), 2 + parity
                )

        def collided(q, low, high):
            part = q % 2
            lanes = slice(LANES * part, LANES * part + LANES)
            found = []
            for index in range(3):
                even = gains[index, 0, low:high, lanes]
                odd = gains[index, 1, low:high, lanes]
                found.append(even + odd if q < 2 else even - odd)
            value = grid[q, low:high]
            return value + rate * (found[0] * found[1] - value * found[2])

        flux_x = [jnp.zeros((1, LANES), F32), jnp.zeros((1, LANES), F32)]
        flux_y = [jnp.zeros((1, LANES), F32), jnp.zeros((1, LANES), F32)]
        copies = []
        for side in range(2):
            low, high = side * (PLANE // 2), (side + 1) * (PLANE // 2)
            for pair in range(2):
                values = []
                for part in range(2):
                    q = 2 * pair + part
                    value = collided(q, low, high)
                    post[q, low:high] = value
                    values.append(value)
                    flux_x[side] = flux_x[side] + jnp.sum(
                        value * rows[0, low:high], axis=0, keepdims=True
                    )
                    flux_y[pair] = flux_y[pair] + lanes_ref[part : part + 1] * jnp.sum(
                        value, axis=0, keepdims=True
                    )
                if side == 0:
                    packed = jnp.where(first_column, values[1], roll(values[0], SY))
                else:
                    packed = jnp.where(first_column, roll(values[0], -SY), values[1])
                halo_out[2 * step + side, pair] = packed
            copy = pltpu.make_async_remote_copy(
                src_ref=halo_out.at[2 * step + side],
                dst_ref=halo_in.at[2 * step + side],
                send_sem=halo_send.at[2 * step + side],
                recv_sem=halo_recv.at[2 * step + side],
                device_id=left_device if side == 0 else right_device,
                device_id_type=MESH,
            )
            copy.start()
            copies.append(copy)

        def over_chunks(value):
            value = value + roll(value, 64)
            return value + roll(value, 32)

        flux = [over_chunks(f) for f in flux_x + flux_y]
        for side in range(2):
            low, high = side * (PLANE // 2), (side + 1) * (PLANE // 2)
            copies[side].wait()
            for pair in range(2):
                packed = halo_in[2 * step + side, pair]
                for part in range(2):
                    q = 2 * pair + part
                    center = post[q, low:high]
                    mirror = post[2 * (1 - pair) + part, low:high]
                    gauss_y = lanes_ref[2 + part : 3 + part]
                    if side == 0:
                        edge = packed if part == 0 else roll(packed, SY)
                        across = jnp.where(first_column, roll(center, -SY), edge)
                        solid = right_solid
                        scale = flux[1] / norms[1]
                    else:
                        edge = packed if part == 0 else roll(packed, -SY)
                        across = jnp.where(first_column, edge, roll(center, SY))
                        solid = left_solid
                        scale = flux[0] / norms[0]
                    rest = rows[1, low:high]
                    across = jnp.where(solid, rest * (scale * gauss_y), across)
                    if pair == 0:
                        ghost = (1.0 - ACC_TOP) * mirror + rows[2, low:high] * (
                            flux[3] * (gauss_y * (ACC_TOP / norms[3]))
                        )
                        along = jnp.where(top_wall, ghost, roll(center, -1))
                    else:
                        ghost = (1.0 - accommodation) * mirror + rest * (
                            accommodation * flux[2] * (gauss_y / norms[2])
                        )
                        along = jnp.where(below_solid, ghost, roll(center, 1))
                    change = rows[0, low:high] * (center - across) + lanes_ref[
                        part : part + 1
                    ] * (center - along)
                    grid[q, low:high] = (center - dt * change) * fluid

    def homeward(position):
        v, s = place_of(position)
        return pltpu.make_async_remote_copy(
            src_ref=grid.at[pl.ds(2 * s, 2), pl.ds(v * depth, depth), :],
            dst_ref=back.at[me],
            send_sem=back_send.at[position],
            recv_sem=back_recv.at[me],
            device_id=device_of(position),
            device_id_type=MESH,
        )

    @pl.loop(0, blocks)
    def _(turn):
        for index in range(4):
            position = 4 * far_first(turn) + index

            @pl.when(position != me)
            def _():
                homeward(position).start()

    own_back = pltpu.make_async_copy(
        grid.at[pl.ds(2 * sub, 2), pl.ds(vel * depth, depth), :], back.at[me], own_sem.at[1]
    )
    own_back.start()

    @pl.loop(1, devices)
    def _(offset):
        outward((me + offset) % devices).wait_send()

    own_back.wait()

    @pl.loop(1, devices)
    def _(offset):
        source = (me + devices - offset) % devices
        pltpu.make_async_remote_copy(
            src_ref=stage.at[source],
            dst_ref=back.at[source],
            send_sem=back_send.at[source],
            recv_sem=back_recv.at[source],
            device_id=device_of(source),
            device_id_type=MESH,
        ).wait_recv()

    @pl.loop(0, devices // 4)
    def _(block):
        start = pl.multiple_of(block * LANES, LANES)
        for part in range(2):
            pieces = [back[4 * block + index, part] for index in range(4)]
            for index, piece in enumerate(chunk_transpose(pieces, low_pair, even_chunk)):
                m = 4 * part + index
                y = m + sub * (HALF - 1 - 2 * m)
                out_ref[y, :, pl.ds(start, LANES)] = piece

    @pl.loop(1, devices)
    def _(offset):
        homeward((me + offset) % devices).wait_send()


def solution(mesh):
    vel_count = mesh.shape["vel"]
    devices = 2 * vel_count
    forward, inverse, height, tables, rows, lanes, dt, norms = constants()
    depth = PLANE // vel_count

    def local(dist, cell_type, groove_mask):
        hbm = pl.BlockSpec(memory_space=pl.ANY)
        vmem = pl.BlockSpec(memory_space=pltpu.VMEM)
        smem = pl.BlockSpec(memory_space=pltpu.SMEM)
        dma = pltpu.SemaphoreType.DMA
        piece = (2, depth, LANES)
        return pl.pallas_call(
            functools.partial(kernel, vel_count, dt, norms),
            out_shape=jax.ShapeDtypeStruct(dist.shape, F32),
            in_specs=[smem, smem, hbm, hbm, hbm, hbm, hbm, hbm, vmem],
            out_specs=vmem,
            scratch_shapes=[
                pltpu.VMEM(dist.shape, F32),
                pltpu.VMEM((devices,) + piece, F32),
                pltpu.VMEM((devices,) + piece, F32),
                pltpu.VMEM((4, PLANE, LANES), F32),
                pltpu.VMEM((4, PLANE, LANES), F32),
                pltpu.VMEM((3, 2, PLANE, PLANE), F32),
                pltpu.VMEM((2 * STEPS, 2, PLANE // 2, LANES), F32),
                pltpu.VMEM((2 * STEPS, 2, PLANE // 2, LANES), F32),
                pltpu.VMEM(forward.shape, BF16),
                pltpu.VMEM(inverse.shape, BF16),
                pltpu.VMEM(height.shape, BF16),
                pltpu.VMEM(tables.shape, F32),
                pltpu.VMEM(rows.shape, F32),
                dma((5,)),
                dma((3,)),
                dma((devices,)),
                dma((devices,)),
                dma((2 * STEPS,)),
                dma((2 * STEPS,)),
                dma((devices,)),
                dma((devices,)),
            ],
            compiler_params=pltpu.CompilerParams(
                collective_id=0, has_side_effects=True, vmem_limit_bytes=60 * 1024 * 1024
            ),
        )(
            cell_type, groove_mask, dist,
            jnp.asarray(forward), jnp.asarray(inverse), jnp.asarray(height),
            jnp.asarray(tables), jnp.asarray(rows), jnp.asarray(lanes),
        )

    return jax.shard_map(
        local,
        mesh=mesh,
        in_specs=(P("sub", "vel", "groups"), P("groups"), P("groups")),
        out_specs=P("sub", "vel", "groups"),
        check_vma=False,
    )
```

```python
import functools
import math

import jax
import jax.numpy as jnp
import numpy as np
from jax import lax
from jax.experimental import pallas as pl
from jax.experimental.pallas import tpu as pltpu
from jax.sharding import PartitionSpec as P

VN = 16
SY = 16
STEPS = 2

VEL_RANGE = 5.0
TOP_SPEED = 1.0
ACC_LAND = 0.4
ACC_TOP = 0.7
KNUDSEN = 1.0
HALF = VN // 2
PLANE = VN * VN
LANES = 128
MESH = pl.DeviceIdType.MESH
F32 = jnp.float32
BF16 = jnp.bfloat16


def real_basis():
    place = np.arange(VN) - (VN - 1) / 2.0
    modes = np.concatenate([np.arange(HALF), np.arange(1, HALF + 1)])
    rows = []
    for index, mode in enumerate(modes):
        angle = 2.0 * math.pi * mode * place / VN
        row = np.cos(angle) if index < HALF else np.sin(angle)
        rows.append(row / np.sqrt(np.sum(row * row)))
    return modes, np.stack(rows)


def halves(table):
    high = table.astype(np.float32).astype(jnp.bfloat16)
    low = (table - high.astype(np.float64)).astype(jnp.bfloat16)
    return high, low


def left_table(table):
    high, low = halves(table)
    return np.concatenate([high, high, low], axis=1)


def right_table(table):
    high, low = halves(table)
    return np.concatenate([high, high, low], axis=0)


@functools.cache
def constants():
    modes, basis = real_basis()
    step = 2.0 * VEL_RANGE / VN
    plane = np.kron(basis, basis)
    order = np.concatenate([np.arange(HALF), np.arange(VN - 1, HALF - 1, -1)])
    across = np.kron(basis[:, order].T, np.eye(SY))
    forward = left_table(plane)
    inverse = left_table(plane.T)
    height = np.stack([right_table(across), right_table(across.T)])
    wave = modes * (math.pi / VEL_RANGE)
    along_y = wave[:, None, None]
    along_x = wave[None, :, None]
    along_z = wave[None, None, :]
    square = along_y**2 + along_x**2 + along_z**2
    first = 1.0 / (1.0 + square / 12.0)
    second = 3.0 * np.cos(0.9 * along_x) / (1.0 + square / 10.0)
    loss = 3.0 / (1.0 + square / 9.0) ** 2
    tables = []
    for table in (first, second, loss):
        tables.append(np.repeat(table.reshape(VN, PLANE).T, SY, axis=1))
    tables = np.stack(tables).astype(np.float32)

    speed = (np.arange(VN) - (VN - 1) / 2.0) * step
    dt = 0.8 / ((VN - 1) * step)
    gauss = np.exp(-speed * speed / 2.0)
    moving = np.exp(-((speed - TOP_SPEED) ** 2) / 2.0)
    speed_x = np.repeat(speed, VN)
    rows = np.stack([np.abs(speed_x), np.kron(gauss, gauss), np.kron(moving, gauss)])
    rows = np.broadcast_to(rows[:, :, None], (3, PLANE, LANES)).astype(np.float32)
    lanes = np.zeros((8, LANES))
    lanes[0] = np.repeat(np.abs(speed[:HALF]), SY)
    lanes[1] = np.repeat(gauss[:HALF], SY)
    up = np.sum(np.maximum(speed, 0.0) * gauss)
    total = np.sum(gauss)
    norms = (
        up * total * total,
        up * total * total,
        up * total * total,
        up * np.sum(moving) * total,
    )
    return forward, inverse, height, tables, rows, lanes.astype(np.float32), dt, norms


def roll(value, shift):
    return pltpu.roll(value, shift % LANES, 1)


def chunk_transpose(parts, lane):
    parts = list(parts)
    for bit in (4, 2, 1):
        width = bit * SY
        first = lane % (2 * width) < width
        for index in range(HALF):
            if index & bit == 0:
                a, b = parts[index], parts[index + bit]
                parts[index] = jnp.where(first, a, roll(b, width))
                parts[index + bit] = jnp.where(first, roll(a, -width), b)
    return parts


def split(value):
    high = value.astype(BF16)
    low = (value - high.astype(F32)).astype(BF16)
    return high, low


def kernel(
    vel_count, dt, norms,
    cell_ref, groove_ref, dist_hbm, forward_hbm, inverse_hbm, height_hbm, tables_hbm, rows_hbm,
    lanes_ref, out_ref,
    dist_ref, stage, back, grid, post, gains, halo_in, forward, inverse, height, tables, rows,
    table_sem, own_sem, send_sem, recv_sem, halo_send, halo_recv, back_send, back_recv,
):
    devices = 2 * vel_count
    depth = dist_ref.shape[1]
    fetch = pltpu.make_async_copy(dist_hbm, dist_ref, own_sem.at[4])
    fetch.start()
    group = lax.axis_index("groups")
    vel = lax.axis_index("vel")
    sub = lax.axis_index("sub")
    ring = vel // 2 + (vel % 2) * (vel_count - 1 - 2 * (vel // 2))
    me = 2 * ring + sub

    def place_of(position):
        index = position // 2
        far = index // (vel_count // 2)
        return 2 * index + far * (2 * (vel_count - 1 - index) + 1 - 2 * index), position % 2

    def device_of(position):
        v, s = place_of(position)
        return (group, v, s)

    loads = [
        pltpu.make_async_copy(source, target, table_sem.at[index])
        for index, (source, target) in enumerate(
            (
                (forward_hbm, forward),
                (inverse_hbm, inverse),
                (height_hbm, height),
                (tables_hbm, tables),
                (rows_hbm, rows),
            )
        )
    ]
    for load in loads:
        load.start()

    barrier = pltpu.get_barrier_semaphore()

    @pl.loop(1, devices)
    def _(offset):
        pl.semaphore_signal(
            barrier, inc=1, device_id=device_of((me + offset) % devices), device_id_type=MESH
        )

    pl.semaphore_wait(barrier, devices - 1)
    fetch.wait()

    lane = lax.broadcasted_iota(jnp.int32, (1, LANES), 1)
    level = lane % SY

    blocks = devices // 4
    mine = me // 4

    def far_first(turn):
        ahead = 1 - 2 * (mine % 2)
        return (mine + ahead * (1 + turn) + 2 * blocks) % blocks

    def outward(column, position):
        return pltpu.make_async_remote_copy(
            src_ref=stage.at[column, position],
            dst_ref=grid.at[column, sub, pl.ds(vel * depth, depth), :],
            send_sem=send_sem.at[column, position],
            recv_sem=recv_sem.at[column, me],
            device_id=device_of(position),
            device_id_type=MESH,
        )

    def send_block(column, block, copy_of):
        for index in range(4):
            position = 4 * block + index

            @pl.when(position != me)
            def _():
                copy_of(column, position).start()

    @pl.loop(0, blocks)
    def _(turn):
        block = far_first(turn)
        start = pl.multiple_of(block * LANES, LANES)
        pieces = []
        for m in range(HALF):
            y = m + sub * (HALF - 1 - 2 * m)
            pieces.append(dist_ref[y, :, pl.ds(start, LANES)])
        for index, piece in enumerate(chunk_transpose(pieces, lane)):
            stage[index % 2, 4 * block + index // 2] = piece
        send_block(0, block, outward)

    @pl.loop(0, blocks)
    def _(turn):
        send_block(1, far_first(turn), outward)

    own = [
        pltpu.make_async_copy(
            stage.at[column, me],
            grid.at[column, sub, pl.ds(vel * depth, depth), :],
            own_sem.at[column],
        )
        for column in range(2)
    ]
    for copy in own:
        copy.start()

    def solid_count(column):
        count = jnp.int32(0)
        for index in range(SY):
            count = count + cell_ref[column * SY + index]
        return count

    columns = 2 * devices
    counts = [solid_count((2 * me + shift + columns) % columns) for shift in range(-1, 3)]
    top_wall = level == SY - 1

    for load in loads:
        load.wait()

    def inward(column, source):
        v, s = place_of(source)
        return pltpu.make_async_remote_copy(
            src_ref=stage.at[column, source],
            dst_ref=grid.at[column, s, pl.ds(v * depth, depth), :],
            send_sem=send_sem.at[column, source],
            recv_sem=recv_sem.at[column, source],
            device_id=device_of(source),
            device_id_type=MESH,
        )

    def homeward(column, position):
        v, s = place_of(position)
        return pltpu.make_async_remote_copy(
            src_ref=grid.at[column, s, pl.ds(v * depth, depth), :],
            dst_ref=back.at[column, me],
            send_sem=back_send.at[column, position],
            recv_sem=back_recv.at[column, me],
            device_id=device_of(position),
            device_id_type=MESH,
        )

    rate = dt / KNUDSEN
    right_device = device_of((me + 1) % devices)
    left_device = device_of((me + devices - 1) % devices)

    def by_height(value, index):
        high, low = split(value)
        return jnp.dot(
            jnp.concatenate([high, low, high], axis=1), height[index], preferred_element_type=F32
        )

    def by_plane(table, value):
        high, low = split(value)
        return jnp.dot(
            table[...], jnp.concatenate([high, low, high], axis=0), preferred_element_type=F32
        )

    sides = (slice(0, PLANE // 2), slice(PLANE // 2, PLANE))

    @pl.loop(0, STEPS)
    def _(step):
        fluxes = []
        copies = []
        for column in range(2):

            @pl.when(step == 0)
            def _():
                own[column].wait()

                @pl.loop(1, devices)
                def _(offset):
                    inward(column, (me + devices - offset) % devices).wait_recv()

            whole = jnp.concatenate([grid[column, 0], grid[column, 1]], axis=1)
            spectrum = by_plane(forward, by_height(whole, 0))
            for index in range(3):
                gains[index] = by_height(by_plane(inverse, spectrum * tables[index]), 1)
            flux = [jnp.zeros((1, LANES), F32) for _ in range(4)]
            for side in range(2):
                for half in range(2):
                    part = slice(half * LANES, (half + 1) * LANES)
                    value = grid[column, half, sides[side]]
                    value = value + rate * (
                        gains[0, sides[side], part] * gains[1, sides[side], part]
                        - value * gains[2, sides[side], part]
                    )
                    post[column, half, sides[side]] = value
                    flux[side] = flux[side] + jnp.sum(
                        value * rows[0, sides[side]], axis=0, keepdims=True
                    )
                    flux[2 + half] = flux[2 + half] + lanes_ref[0:1] * jnp.sum(
                        value, axis=0, keepdims=True
                    )
            for index in range(4):
                for width in (64, 32, 16):
                    flux[index] = flux[index] + roll(flux[index], width)
            fluxes.append(flux)
            copy = pltpu.make_async_remote_copy(
                src_ref=post.at[column, :, sides[column], :],
                dst_ref=halo_in.at[2 * step + column],
                send_sem=halo_send.at[2 * step + column],
                recv_sem=halo_recv.at[2 * step + column],
                device_id=left_device if column == 0 else right_device,
                device_id_type=MESH,
            )
            copy.start()
            copies.append(copy)

        speed_y, gauss_y = lanes_ref[0:1], lanes_ref[1:2]
        for column in range(2):
            flux = fluxes[column]
            count = counts[1 + column]
            fluid = jnp.where(level < count, 0.0, 1.0)
            below_solid = level <= count
            groove = groove_ref[2 * me + column]
            accommodation = jnp.where(groove == 1, F32(1.0), F32(ACC_LAND))
            for side in (column, 1 - column):
                solid = level < counts[2 + column if side == 0 else column]
                scale = flux[1 - side] * (gauss_y / norms[1 - side])
                if side != column:
                    copies[side].wait()
                for half in range(2):
                    center = post[column, half, sides[side]]
                    mirror = post[column, 1 - half, sides[side]]
                    if side == column:
                        across = post[1 - column, half, sides[side]]
                    else:
                        across = halo_in[2 * step + side, half]
                    across = jnp.where(solid, rows[1, sides[side]] * scale, across)
                    if half == 0:
                        ghost = (1.0 - ACC_TOP) * mirror + rows[2, sides[side]] * (
                            flux[3] * (gauss_y * (ACC_TOP / norms[3]))
                        )
                        along = jnp.where(top_wall, ghost, roll(center, -1))
                    else:
                        ghost = (1.0 - accommodation) * mirror + rows[1, sides[side]] * (
                            accommodation * flux[2] * (gauss_y / norms[2])
                        )
                        along = jnp.where(below_solid, ghost, roll(center, 1))
                    change = rows[0, sides[side]] * (center - across) + speed_y * (center - along)
                    grid[column, half, sides[side]] = (center - dt * change) * fluid

            @pl.when(step == STEPS - 1)
            def _():
                @pl.loop(0, blocks)
                def _(turn):
                    send_block(column, far_first(turn), homeward)

    own_back = [
        pltpu.make_async_copy(
            grid.at[column, sub, pl.ds(vel * depth, depth), :],
            back.at[column, me],
            own_sem.at[2 + column],
        )
        for column in range(2)
    ]
    for copy in own_back:
        copy.start()
    for column in range(2):

        @pl.loop(1, devices)
        def _(offset):
            outward(column, (me + offset) % devices).wait_send()

    for copy in own_back:
        copy.wait()
    for column in range(2):

        @pl.loop(1, devices)
        def _(offset):
            source = (me + devices - offset) % devices
            pltpu.make_async_remote_copy(
                src_ref=stage.at[column, source],
                dst_ref=back.at[column, source],
                send_sem=back_send.at[column, source],
                recv_sem=back_recv.at[column, source],
                device_id=device_of(source),
                device_id_type=MESH,
            ).wait_recv()

    @pl.loop(0, blocks)
    def _(block):
        start = pl.multiple_of(block * LANES, LANES)
        pieces = [back[index % 2, 4 * block + index // 2] for index in range(HALF)]
        for m, piece in enumerate(chunk_transpose(pieces, lane)):
            y = m + sub * (HALF - 1 - 2 * m)
            out_ref[y, :, pl.ds(start, LANES)] = piece

    for column in range(2):

        @pl.loop(1, devices)
        def _(offset):
            homeward(column, (me + offset) % devices).wait_send()


def solution(mesh):
    vel_count = mesh.shape["vel"]
    devices = 2 * vel_count
    forward, inverse, height, tables, rows, lanes, dt, norms = constants()
    depth = PLANE // vel_count

    def local(dist, cell_type, groove_mask):
        hbm = pl.BlockSpec(memory_space=pl.ANY)
        vmem = pl.BlockSpec(memory_space=pltpu.VMEM)
        smem = pl.BlockSpec(memory_space=pltpu.SMEM)
        dma = pltpu.SemaphoreType.DMA
        piece = (2, devices, depth, LANES)
        return pl.pallas_call(
            functools.partial(kernel, vel_count, dt, norms),
            out_shape=jax.ShapeDtypeStruct(dist.shape, F32),
            in_specs=[smem, smem, hbm, hbm, hbm, hbm, hbm, hbm, vmem],
            out_specs=vmem,
            scratch_shapes=[
                pltpu.VMEM(dist.shape, F32),
                pltpu.VMEM(piece, F32),
                pltpu.VMEM(piece, F32),
                pltpu.VMEM((2, 2, PLANE, LANES), F32),
                pltpu.VMEM((2, 2, PLANE, LANES), F32),
                pltpu.VMEM((3, PLANE, PLANE), F32),
                pltpu.VMEM((2 * STEPS, 2, PLANE // 2, LANES), F32),
                pltpu.VMEM(forward.shape, BF16),
                pltpu.VMEM(inverse.shape, BF16),
                pltpu.VMEM(height.shape, BF16),
                pltpu.VMEM(tables.shape, F32),
                pltpu.VMEM(rows.shape, F32),
                dma((5,)),
                dma((5,)),
                dma((2, devices)),
                dma((2, devices)),
                dma((2 * STEPS,)),
                dma((2 * STEPS,)),
                dma((2, devices)),
                dma((2, devices)),
            ],
            compiler_params=pltpu.CompilerParams(
                collective_id=0, has_side_effects=True, vmem_limit_bytes=60 * 1024 * 1024
            ),
        )(
            cell_type, groove_mask, dist,
            jnp.asarray(forward), jnp.asarray(inverse), jnp.asarray(height),
            jnp.asarray(tables), jnp.asarray(rows), jnp.asarray(lanes),
        )

    return jax.shard_map(
        local,
        mesh=mesh,
        in_specs=(P("sub", "vel", "groups"), P("groups"), P("groups")),
        out_specs=P("sub", "vel", "groups"),
        check_vma=False,
    )
```

```python
import functools
import math

import jax
import jax.numpy as jnp
import numpy as np
from jax import lax
from jax.experimental import pallas as pl
from jax.experimental.pallas import tpu as pltpu
from jax.sharding import PartitionSpec as P

VN = 16
SY = 16
STEPS = 2

VEL_RANGE = 5.0
TOP_SPEED = 1.0
ACC_LAND = 0.4
ACC_TOP = 0.7
KNUDSEN = 1.0
HALF = VN // 2
PLANE = VN * VN
LANES = 128
MESH = pl.DeviceIdType.MESH
F32 = jnp.float32
BF16 = jnp.bfloat16


def real_basis():
    place = np.arange(VN) - (VN - 1) / 2.0
    modes = np.concatenate([np.arange(HALF), np.arange(1, HALF + 1)])
    rows = []
    for index, mode in enumerate(modes):
        angle = 2.0 * math.pi * mode * place / VN
        row = np.cos(angle) if index < HALF else np.sin(angle)
        rows.append(row / np.sqrt(np.sum(row * row)))
    return modes, np.stack(rows)


def halves(table):
    high = table.astype(np.float32).astype(jnp.bfloat16)
    low = (table - high.astype(np.float64)).astype(jnp.bfloat16)
    return high, low


def left_table(table):
    high, low = halves(table)
    return np.concatenate([high, high, low], axis=1)


def right_table(table):
    high, low = halves(table)
    return np.concatenate([high, high, low], axis=0)


@functools.cache
def constants():
    modes, basis = real_basis()
    step = 2.0 * VEL_RANGE / VN
    plane = np.kron(basis, basis)
    order = np.concatenate([np.arange(HALF), np.arange(VN - 1, HALF - 1, -1)])
    across = np.kron(basis[:, order].T, np.eye(SY))
    forward = left_table(plane)
    inverse = left_table(plane.T)
    height = np.stack([right_table(across), right_table(across.T)])
    wave = modes * (math.pi / VEL_RANGE)
    along_y = wave[:, None, None]
    along_x = wave[None, :, None]
    along_z = wave[None, None, :]
    square = along_y**2 + along_x**2 + along_z**2
    first = 1.0 / (1.0 + square / 12.0)
    second = 3.0 * np.cos(0.9 * along_x) / (1.0 + square / 10.0)
    loss = 3.0 / (1.0 + square / 9.0) ** 2
    tables = []
    for table in (first, second, loss):
        tables.append(np.repeat(table.reshape(VN, PLANE).T, SY, axis=1))
    tables = np.stack(tables).astype(np.float32)

    speed = (np.arange(VN) - (VN - 1) / 2.0) * step
    dt = 0.8 / ((VN - 1) * step)
    gauss = np.exp(-speed * speed / 2.0)
    moving = np.exp(-((speed - TOP_SPEED) ** 2) / 2.0)
    speed_x = np.repeat(speed, VN)
    rows = np.stack([np.abs(speed_x), np.kron(gauss, gauss), np.kron(moving, gauss)])
    rows = np.broadcast_to(rows[:, :, None], (3, PLANE, LANES)).astype(np.float32)
    lanes = np.zeros((8, LANES))
    lanes[0] = np.repeat(np.abs(speed[:HALF]), SY)
    lanes[1] = np.repeat(gauss[:HALF], SY)
    up = np.sum(np.maximum(speed, 0.0) * gauss)
    total = np.sum(gauss)
    norms = (
        up * total * total,
        up * total * total,
        up * total * total,
        up * np.sum(moving) * total,
    )
    return forward, inverse, height, tables, rows, lanes.astype(np.float32), dt, norms


def roll(value, shift):
    return pltpu.roll(value, shift % LANES, 1)


def chunk_transpose(parts, lane):
    parts = list(parts)
    for bit in (4, 2, 1):
        width = bit * SY
        first = lane % (2 * width) < width
        for index in range(HALF):
            if index & bit == 0:
                a, b = parts[index], parts[index + bit]
                parts[index] = jnp.where(first, a, roll(b, width))
                parts[index + bit] = jnp.where(first, roll(a, -width), b)
    return parts


def split(value):
    high = value.astype(BF16)
    low = (value - high.astype(F32)).astype(BF16)
    return high, low


def kernel(
    vel_count, dt, norms,
    cell_ref, groove_ref, dist_hbm, forward_hbm, inverse_hbm, height_hbm, tables_hbm, rows_hbm,
    lanes_ref, out_ref,
    dist_ref, stage, back, grid, post, gains, halo_in, forward, inverse, height, tables, rows,
    table_sem, own_sem, send_sem, recv_sem, halo_send, halo_recv, back_send, back_recv,
):
    devices = 2 * vel_count
    depth = dist_ref.shape[1]
    fetch = pltpu.make_async_copy(dist_hbm, dist_ref, own_sem.at[0])
    fetch.start()
    group = lax.axis_index("groups")
    vel = lax.axis_index("vel")
    sub = lax.axis_index("sub")
    ring = vel // 2 + (vel % 2) * (vel_count - 1 - 2 * (vel // 2))
    me = 2 * ring + sub

    def place_of(position):
        index = position // 2
        far = index // (vel_count // 2)
        return 2 * index + far * (2 * (vel_count - 1 - index) + 1 - 2 * index), position % 2

    def device_of(position):
        v, s = place_of(position)
        return (group, v, s)

    loads = [
        pltpu.make_async_copy(source, target, table_sem.at[index])
        for index, (source, target) in enumerate(
            (
                (forward_hbm, forward),
                (inverse_hbm, inverse),
                (height_hbm, height),
                (tables_hbm, tables),
                (rows_hbm, rows),
            )
        )
    ]
    for load in loads:
        load.start()

    barrier = pltpu.get_barrier_semaphore()

    @pl.loop(1, devices)
    def _(offset):
        pl.semaphore_signal(
            barrier, inc=1, device_id=device_of((me + offset) % devices), device_id_type=MESH
        )

    pl.semaphore_wait(barrier, devices - 1)
    fetch.wait()

    lane = lax.broadcasted_iota(jnp.int32, (1, LANES), 1)
    level = lane % SY

    blocks = devices // 4
    mine = me // 4

    def far_first(turn):
        ahead = 1 - 2 * (mine % 2)
        return (mine + ahead * (1 + turn) + 2 * blocks) % blocks

    def outward(column, position):
        return pltpu.make_async_remote_copy(
            src_ref=stage.at[column, position],
            dst_ref=grid.at[column, sub, pl.ds(vel * depth, depth), :],
            send_sem=send_sem.at[column],
            recv_sem=recv_sem.at[column],
            device_id=device_of(position),
            device_id_type=MESH,
        )

    def send_block(column, block, copy_of, side=None):
        for index in range(4):
            position = 4 * block + index
            wanted = position != me
            if side is not None:
                wanted &= place_of(position)[0] // (vel_count // 2) == side

            @pl.when(wanted)
            def _():
                copy_of(column, position).start()

    @pl.loop(0, blocks)
    def _(turn):
        block = far_first(turn)
        start = pl.multiple_of(block * LANES, LANES)
        pieces = []
        for m in range(HALF):
            y = m + sub * (HALF - 1 - 2 * m)
            pieces.append(dist_ref[y, :, pl.ds(start, LANES)])
        for index, piece in enumerate(chunk_transpose(pieces, lane)):
            stage[index % 2, 4 * block + index // 2] = piece
        send_block(0, block, outward)

    @pl.loop(0, blocks)
    def _(turn):
        send_block(1, far_first(turn), outward)

    own = [
        pltpu.make_async_copy(
            stage.at[column, me],
            grid.at[column, sub, pl.ds(vel * depth, depth), :],
            recv_sem.at[column],
        )
        for column in range(2)
    ]
    for copy in own:
        copy.start()

    def solid_count(column):
        count = jnp.int32(0)
        for index in range(SY):
            count = count + cell_ref[column * SY + index]
        return count

    columns = 2 * devices
    counts = [solid_count((2 * me + shift + columns) % columns) for shift in range(-1, 3)]
    top_wall = level == SY - 1

    for load in loads:
        load.wait()

    def homeward(column, position):
        v, s = place_of(position)
        return pltpu.make_async_remote_copy(
            src_ref=grid.at[column, s, pl.ds(v * depth, depth), :],
            dst_ref=back.at[column, me],
            send_sem=back_send.at[column],
            recv_sem=back_recv.at[column],
            device_id=device_of(position),
            device_id_type=MESH,
        )

    rate = dt / KNUDSEN
    right_device = device_of((me + 1) % devices)
    left_device = device_of((me + devices - 1) % devices)

    def by_height(value, index):
        high, low = split(value)
        return jnp.dot(
            jnp.concatenate([high, low, high], axis=1), height[index], preferred_element_type=F32
        )

    def by_plane(table, value):
        high, low = split(value)
        return jnp.dot(
            table[...], jnp.concatenate([high, low, high], axis=0), preferred_element_type=F32
        )

    sides = (slice(0, PLANE // 2), slice(PLANE // 2, PLANE))

    @pl.loop(0, STEPS)
    def _(step):
        fluxes = []
        copies = []
        for column in range(2):

            @pl.when(step == 0)
            def _():
                pltpu.make_async_copy(grid.at[column], grid.at[column], recv_sem.at[column]).wait()

            whole = jnp.concatenate([grid[column, 0], grid[column, 1]], axis=1)
            spectrum = by_plane(forward, by_height(whole, 0))
            for index in range(3):
                gains[index] = by_height(by_plane(inverse, spectrum * tables[index]), 1)
            flux = [jnp.zeros((1, LANES), F32) for _ in range(4)]
            for side in range(2):
                for half in range(2):
                    part = slice(half * LANES, (half + 1) * LANES)
                    value = grid[column, half, sides[side]]
                    value = value + rate * (
                        gains[0, sides[side], part] * gains[1, sides[side], part]
                        - value * gains[2, sides[side], part]
                    )
                    post[column, half, sides[side]] = value
                    flux[side] = flux[side] + jnp.sum(
                        value * rows[0, sides[side]], axis=0, keepdims=True
                    )
                    flux[2 + half] = flux[2 + half] + lanes_ref[0:1] * jnp.sum(
                        value, axis=0, keepdims=True
                    )
            for index in range(4):
                for width in (64, 32, 16):
                    flux[index] = flux[index] + roll(flux[index], width)
            fluxes.append(flux)
            copy = pltpu.make_async_remote_copy(
                src_ref=post.at[column, :, sides[column], :],
                dst_ref=halo_in.at[2 * step + column],
                send_sem=halo_send.at[2 * step + column],
                recv_sem=halo_recv.at[2 * step + column],
                device_id=left_device if column == 0 else right_device,
                device_id_type=MESH,
            )
            copy.start()
            copies.append(copy)

        speed_y, gauss_y = lanes_ref[0:1], lanes_ref[1:2]
        for column, side in ((0, 0), (1, 1), (1, 0), (0, 1)):
            flux = fluxes[column]
            count = counts[1 + column]
            fluid = jnp.where(level < count, 0.0, 1.0)
            below_solid = level <= count
            groove = groove_ref[2 * me + column]
            accommodation = jnp.where(groove == 1, F32(1.0), F32(ACC_LAND))
            solid = level < counts[2 + column if side == 0 else column]
            scale = flux[1 - side] * (gauss_y / norms[1 - side])
            if side != column:
                copies[side].wait()
            for half in range(2):
                center = post[column, half, sides[side]]
                mirror = post[column, 1 - half, sides[side]]
                if side == column:
                    across = post[1 - column, half, sides[side]]
                else:
                    across = halo_in[2 * step + side, half]
                across = jnp.where(solid, rows[1, sides[side]] * scale, across)
                if half == 0:
                    ghost = (1.0 - ACC_TOP) * mirror + rows[2, sides[side]] * (
                        flux[3] * (gauss_y * (ACC_TOP / norms[3]))
                    )
                    along = jnp.where(top_wall, ghost, roll(center, -1))
                else:
                    ghost = (1.0 - accommodation) * mirror + rows[1, sides[side]] * (
                        accommodation * flux[2] * (gauss_y / norms[2])
                    )
                    along = jnp.where(below_solid, ghost, roll(center, 1))
                change = rows[0, sides[side]] * (center - across) + speed_y * (center - along)
                grid[column, half, sides[side]] = (center - dt * change) * fluid

            @pl.when(step == STEPS - 1)
            def _():
                @pl.loop(0, blocks)
                def _(turn):
                    send_block(column, far_first(turn), homeward, side)

    for column in range(2):
        pltpu.make_async_copy(
            grid.at[column, sub, pl.ds(vel * depth, depth), :],
            back.at[column, me],
            back_recv.at[column],
        ).start()
    for column in range(2):
        pltpu.make_async_copy(back.at[column], back.at[column], back_recv.at[column]).wait()

    @pl.loop(0, blocks)
    def _(block):
        start = pl.multiple_of(block * LANES, LANES)
        pieces = [back[index % 2, 4 * block + index // 2] for index in range(HALF)]
        for m, piece in enumerate(chunk_transpose(pieces, lane)):
            y = m + sub * (HALF - 1 - 2 * m)
            out_ref[y, :, pl.ds(start, LANES)] = piece

    for column in range(2):
        for sem in (send_sem, back_send):
            sent = stage.at[column, pl.ds(0, devices - 1)]
            pltpu.make_async_copy(sent, sent, sem.at[column]).wait()


def solution(mesh):
    vel_count = mesh.shape["vel"]
    devices = 2 * vel_count
    forward, inverse, height, tables, rows, lanes, dt, norms = constants()
    depth = PLANE // vel_count

    def local(dist, cell_type, groove_mask):
        hbm = pl.BlockSpec(memory_space=pl.ANY)
        vmem = pl.BlockSpec(memory_space=pltpu.VMEM)
        smem = pl.BlockSpec(memory_space=pltpu.SMEM)
        dma = pltpu.SemaphoreType.DMA
        piece = (2, devices, depth, LANES)
        return pl.pallas_call(
            functools.partial(kernel, vel_count, dt, norms),
            out_shape=jax.ShapeDtypeStruct(dist.shape, F32),
            in_specs=[smem, smem, hbm, hbm, hbm, hbm, hbm, hbm, vmem],
            out_specs=vmem,
            scratch_shapes=[
                pltpu.VMEM(dist.shape, F32),
                pltpu.VMEM(piece, F32),
                pltpu.VMEM(piece, F32),
                pltpu.VMEM((2, 2, PLANE, LANES), F32),
                pltpu.VMEM((2, 2, PLANE, LANES), F32),
                pltpu.VMEM((3, PLANE, PLANE), F32),
                pltpu.VMEM((2 * STEPS, 2, PLANE // 2, LANES), F32),
                pltpu.VMEM(forward.shape, BF16),
                pltpu.VMEM(inverse.shape, BF16),
                pltpu.VMEM(height.shape, BF16),
                pltpu.VMEM(tables.shape, F32),
                pltpu.VMEM(rows.shape, F32),
                dma((5,)),
                dma((1,)),
                dma((2,)),
                dma((2,)),
                dma((2 * STEPS,)),
                dma((2 * STEPS,)),
                dma((2,)),
                dma((2,)),
            ],
            compiler_params=pltpu.CompilerParams(
                collective_id=0, has_side_effects=True, vmem_limit_bytes=60 * 1024 * 1024
            ),
        )(
            cell_type, groove_mask, dist,
            jnp.asarray(forward), jnp.asarray(inverse), jnp.asarray(height),
            jnp.asarray(tables), jnp.asarray(rows), jnp.asarray(lanes),
        )

    return jax.shard_map(
        local,
        mesh=mesh,
        in_specs=(P("sub", "vel", "groups"), P("groups"), P("groups")),
        out_specs=P("sub", "vel", "groups"),
        check_vma=False,
    )
```

```python
import functools
import math

import jax
import jax.numpy as jnp
import numpy as np
from jax import lax
from jax.experimental import pallas as pl
from jax.experimental.pallas import tpu as pltpu
from jax.sharding import PartitionSpec as P

VN = 16
SY = 16
STEPS = 2

VEL_RANGE = 5.0
TOP_SPEED = 1.0
ACC_LAND = 0.4
ACC_TOP = 0.7
KNUDSEN = 1.0
HALF = VN // 2
PLANE = VN * VN
LANES = 128
MESH = pl.DeviceIdType.MESH
F32 = jnp.float32
BF16 = jnp.bfloat16


def real_basis():
    place = np.arange(VN) - (VN - 1) / 2.0
    modes = np.concatenate([np.arange(HALF), np.arange(1, HALF + 1)])
    rows = []
    for index, mode in enumerate(modes):
        angle = 2.0 * math.pi * mode * place / VN
        row = np.cos(angle) if index < HALF else np.sin(angle)
        rows.append(row / np.sqrt(np.sum(row * row)))
    return modes, np.stack(rows)


def halves(table):
    high = table.astype(np.float32).astype(jnp.bfloat16)
    low = (table - high.astype(np.float64)).astype(jnp.bfloat16)
    return high, low


def left_table(table):
    high, low = halves(table)
    return np.concatenate([high, high, low], axis=1)


def right_table(table):
    high, low = halves(table)
    return np.concatenate([high, high, low], axis=0)


@functools.cache
def constants():
    modes, basis = real_basis()
    step = 2.0 * VEL_RANGE / VN
    plane = np.kron(basis, basis)
    order = np.concatenate([np.arange(HALF), np.arange(VN - 1, HALF - 1, -1)])
    across = np.kron(basis[:, order].T, np.eye(SY))
    forward = left_table(plane)
    inverse = left_table(plane.T)
    height = np.stack([right_table(across), right_table(across.T)])
    wave = modes * (math.pi / VEL_RANGE)
    along_y = wave[:, None, None]
    along_x = wave[None, :, None]
    along_z = wave[None, None, :]
    square = along_y**2 + along_x**2 + along_z**2
    first = 1.0 / (1.0 + square / 12.0)
    second = 3.0 * np.cos(0.9 * along_x) / (1.0 + square / 10.0)
    loss = 3.0 / (1.0 + square / 9.0) ** 2
    tables = []
    for table in (first, second, loss):
        tables.append(np.repeat(table.reshape(VN, PLANE).T, SY, axis=1))
    tables = np.stack(tables).astype(np.float32)

    speed = (np.arange(VN) - (VN - 1) / 2.0) * step
    dt = 0.8 / ((VN - 1) * step)
    gauss = np.exp(-speed * speed / 2.0)
    moving = np.exp(-((speed - TOP_SPEED) ** 2) / 2.0)
    speed_x = np.repeat(speed, VN)
    rows = np.stack([np.abs(speed_x), np.kron(gauss, gauss), np.kron(moving, gauss)])
    rows = np.broadcast_to(rows[:, :, None], (3, PLANE, LANES)).astype(np.float32)
    lanes = np.zeros((8, LANES))
    lanes[0] = np.repeat(np.abs(speed[:HALF]), SY)
    lanes[1] = np.repeat(gauss[:HALF], SY)
    up = np.sum(np.maximum(speed, 0.0) * gauss)
    total = np.sum(gauss)
    norms = (
        up * total * total,
        up * total * total,
        up * total * total,
        up * np.sum(moving) * total,
    )
    return forward, inverse, height, tables, rows, lanes.astype(np.float32), dt, norms


def roll(value, shift):
    return pltpu.roll(value, shift % LANES, 1)


def chunk_transpose(parts, lane):
    parts = list(parts)
    for bit in (4, 2, 1):
        width = bit * SY
        first = lane % (2 * width) < width
        for index in range(HALF):
            if index & bit == 0:
                a, b = parts[index], parts[index + bit]
                parts[index] = jnp.where(first, a, roll(b, width))
                parts[index + bit] = jnp.where(first, roll(a, -width), b)
    return parts


def split(value):
    high = value.astype(BF16)
    low = (value - high.astype(F32)).astype(BF16)
    return high, low


def kernel(
    vel_count, dt, norms,
    cell_ref, groove_ref, dist_hbm, forward_hbm, inverse_hbm, height_hbm, tables_hbm, rows_hbm,
    lanes_ref, out_ref,
    dist_ref, stage, back, grid, post, gains, halo_in, forward, inverse, height, tables, rows,
    table_sem, own_sem, send_sem, recv_sem, halo_send, halo_recv, back_send, back_recv,
):
    devices = 2 * vel_count
    depth = dist_ref.shape[1]
    fetch = pltpu.make_async_copy(dist_hbm, dist_ref, own_sem.at[0])
    fetch.start()
    group = lax.axis_index("groups")
    vel = lax.axis_index("vel")
    sub = lax.axis_index("sub")
    ring = vel // 2 + (vel % 2) * (vel_count - 1 - 2 * (vel // 2))
    me = 2 * ring + sub

    def place_of(position):
        index = position // 2
        far = index // (vel_count // 2)
        return 2 * index + far * (2 * (vel_count - 1 - index) + 1 - 2 * index), position % 2

    def device_of(position):
        v, s = place_of(position)
        return (group, v, s)

    loads = [
        pltpu.make_async_copy(source, target, table_sem.at[index])
        for index, (source, target) in enumerate(
            (
                (forward_hbm, forward),
                (inverse_hbm, inverse),
                (height_hbm, height),
                (tables_hbm, tables),
                (rows_hbm, rows),
            )
        )
    ]
    for load in loads:
        load.start()

    barrier = pltpu.get_barrier_semaphore()

    @pl.loop(1, devices)
    def _(offset):
        pl.semaphore_signal(
            barrier, inc=1, device_id=device_of((me + offset) % devices), device_id_type=MESH
        )

    fetch.wait()

    lane = lax.broadcasted_iota(jnp.int32, (1, LANES), 1)
    level = lane % SY

    blocks = devices // 4
    mine = me // 4

    def far_first(turn):
        ahead = 1 - 2 * (mine % 2)
        return (mine + ahead * (1 + turn) + 2 * blocks) % blocks

    def outward(column, position):
        return pltpu.make_async_remote_copy(
            src_ref=stage.at[column, position],
            dst_ref=grid.at[column, sub, pl.ds(vel * depth, depth), :],
            send_sem=send_sem.at[column],
            recv_sem=recv_sem.at[column],
            device_id=device_of(position),
            device_id_type=MESH,
        )

    def send_block(column, block, copy_of, side=None):
        for index in range(4):
            position = 4 * block + index
            wanted = position != me
            if side is not None:
                wanted &= place_of(position)[0] // (vel_count // 2) == side

            @pl.when(wanted)
            def _():
                copy_of(column, position).start()

    @pl.loop(0, blocks, unroll=4)
    def _(turn):
        block = far_first(turn)
        start = pl.multiple_of(block * LANES, LANES)
        pieces = []
        for m in range(HALF):
            y = m + sub * (HALF - 1 - 2 * m)
            pieces.append(dist_ref[y, :, pl.ds(start, LANES)])
        for index, piece in enumerate(chunk_transpose(pieces, lane)):
            stage[index % 2, 4 * block + index // 2] = piece

    pl.semaphore_wait(barrier, devices - 1)
    for column in range(2):

        @pl.loop(0, blocks)
        def _(turn):
            send_block(column, far_first(turn), outward)

    own = [
        pltpu.make_async_copy(
            stage.at[column, me],
            grid.at[column, sub, pl.ds(vel * depth, depth), :],
            recv_sem.at[column],
        )
        for column in range(2)
    ]
    for copy in own:
        copy.start()

    def solid_count(column):
        count = jnp.int32(0)
        for index in range(SY):
            count = count + cell_ref[column * SY + index]
        return count

    columns = 2 * devices
    counts = [solid_count((2 * me + shift + columns) % columns) for shift in range(-1, 3)]
    top_wall = level == SY - 1

    for load in loads:
        load.wait()

    def homeward(column, position):
        v, s = place_of(position)
        return pltpu.make_async_remote_copy(
            src_ref=grid.at[column, s, pl.ds(v * depth, depth), :],
            dst_ref=back.at[column, me],
            send_sem=back_send.at[column],
            recv_sem=back_recv.at[column],
            device_id=device_of(position),
            device_id_type=MESH,
        )

    rate = dt / KNUDSEN
    right_device = device_of((me + 1) % devices)
    left_device = device_of((me + devices - 1) % devices)

    def by_height(value, index):
        high, low = split(value)
        return jnp.dot(
            jnp.concatenate([high, low, high], axis=1), height[index], preferred_element_type=F32
        )

    def by_plane(table, value):
        high, low = split(value)
        return jnp.dot(
            table[...], jnp.concatenate([high, low, high], axis=0), preferred_element_type=F32
        )

    sides = (slice(0, PLANE // 2), slice(PLANE // 2, PLANE))

    @pl.loop(0, STEPS)
    def _(step):
        fluxes = []
        copies = []
        for column in range(2):

            @pl.when(step == 0)
            def _():
                pltpu.make_async_copy(grid.at[column], grid.at[column], recv_sem.at[column]).wait()

            whole = jnp.concatenate([grid[column, 0], grid[column, 1]], axis=1)
            spectrum = by_plane(forward, by_height(whole, 0))
            for index in range(3):
                gains[index] = by_height(by_plane(inverse, spectrum * tables[index]), 1)
            flux = [jnp.zeros((1, LANES), F32) for _ in range(4)]
            for side in range(2):
                for half in range(2):
                    part = slice(half * LANES, (half + 1) * LANES)
                    value = grid[column, half, sides[side]]
                    value = value + rate * (
                        gains[0, sides[side], part] * gains[1, sides[side], part]
                        - value * gains[2, sides[side], part]
                    )
                    post[column, half, sides[side]] = value
                    flux[side] = flux[side] + jnp.sum(
                        value * rows[0, sides[side]], axis=0, keepdims=True
                    )
                    flux[2 + half] = flux[2 + half] + lanes_ref[0:1] * jnp.sum(
                        value, axis=0, keepdims=True
                    )
            for index in range(4):
                for width in (64, 32, 16):
                    flux[index] = flux[index] + roll(flux[index], width)
            fluxes.append(flux)
            copy = pltpu.make_async_remote_copy(
                src_ref=post.at[column, :, sides[column], :],
                dst_ref=halo_in.at[2 * step + column],
                send_sem=halo_send.at[2 * step + column],
                recv_sem=halo_recv.at[2 * step + column],
                device_id=left_device if column == 0 else right_device,
                device_id_type=MESH,
            )
            copy.start()
            copies.append(copy)

        speed_y, gauss_y = lanes_ref[0:1], lanes_ref[1:2]
        for column, side in ((0, 0), (1, 1), (1, 0), (0, 1)):
            flux = fluxes[column]
            count = counts[1 + column]
            fluid = jnp.where(level < count, 0.0, 1.0)
            below_solid = level <= count
            groove = groove_ref[2 * me + column]
            accommodation = jnp.where(groove == 1, F32(1.0), F32(ACC_LAND))
            solid = level < counts[2 + column if side == 0 else column]
            scale = flux[1 - side] * (gauss_y / norms[1 - side])
            if side != column:
                copies[side].wait()
            for half in range(2):
                center = post[column, half, sides[side]]
                mirror = post[column, 1 - half, sides[side]]
                if side == column:
                    across = post[1 - column, half, sides[side]]
                else:
                    across = halo_in[2 * step + side, half]
                across = jnp.where(solid, rows[1, sides[side]] * scale, across)
                if half == 0:
                    ghost = (1.0 - ACC_TOP) * mirror + rows[2, sides[side]] * (
                        flux[3] * (gauss_y * (ACC_TOP / norms[3]))
                    )
                    along = jnp.where(top_wall, ghost, roll(center, -1))
                else:
                    ghost = (1.0 - accommodation) * mirror + rows[1, sides[side]] * (
                        accommodation * flux[2] * (gauss_y / norms[2])
                    )
                    along = jnp.where(below_solid, ghost, roll(center, 1))
                change = rows[0, sides[side]] * (center - across) + speed_y * (center - along)
                grid[column, half, sides[side]] = (center - dt * change) * fluid

            @pl.when(step == STEPS - 1)
            def _():
                @pl.loop(0, blocks)
                def _(turn):
                    send_block(column, far_first(turn), homeward, side)

    for column in range(2):
        pltpu.make_async_copy(
            grid.at[column, sub, pl.ds(vel * depth, depth), :],
            back.at[column, me],
            back_recv.at[column],
        ).start()
    for column in range(2):
        pltpu.make_async_copy(back.at[column], back.at[column], back_recv.at[column]).wait()

    @pl.loop(0, blocks, unroll=4)
    def _(block):
        start = pl.multiple_of(block * LANES, LANES)
        pieces = [back[index % 2, 4 * block + index // 2] for index in range(HALF)]
        for m, piece in enumerate(chunk_transpose(pieces, lane)):
            y = m + sub * (HALF - 1 - 2 * m)
            out_ref[y, :, pl.ds(start, LANES)] = piece

    for column in range(2):
        for sem in (send_sem, back_send):
            sent = stage.at[column, pl.ds(0, devices - 1)]
            pltpu.make_async_copy(sent, sent, sem.at[column]).wait()


def solution(mesh):
    vel_count = mesh.shape["vel"]
    devices = 2 * vel_count
    forward, inverse, height, tables, rows, lanes, dt, norms = constants()
    depth = PLANE // vel_count

    def local(dist, cell_type, groove_mask):
        hbm = pl.BlockSpec(memory_space=pl.ANY)
        vmem = pl.BlockSpec(memory_space=pltpu.VMEM)
        smem = pl.BlockSpec(memory_space=pltpu.SMEM)
        dma = pltpu.SemaphoreType.DMA
        piece = (2, devices, depth, LANES)
        return pl.pallas_call(
            functools.partial(kernel, vel_count, dt, norms),
            out_shape=jax.ShapeDtypeStruct(dist.shape, F32),
            in_specs=[smem, smem, hbm, hbm, hbm, hbm, hbm, hbm, vmem],
            out_specs=vmem,
            scratch_shapes=[
                pltpu.VMEM(dist.shape, F32),
                pltpu.VMEM(piece, F32),
                pltpu.VMEM(piece, F32),
                pltpu.VMEM((2, 2, PLANE, LANES), F32),
                pltpu.VMEM((2, 2, PLANE, LANES), F32),
                pltpu.VMEM((3, PLANE, PLANE), F32),
                pltpu.VMEM((2 * STEPS, 2, PLANE // 2, LANES), F32),
                pltpu.VMEM(forward.shape, BF16),
                pltpu.VMEM(inverse.shape, BF16),
                pltpu.VMEM(height.shape, BF16),
                pltpu.VMEM(tables.shape, F32),
                pltpu.VMEM(rows.shape, F32),
                dma((5,)),
                dma((1,)),
                dma((2,)),
                dma((2,)),
                dma((2 * STEPS,)),
                dma((2 * STEPS,)),
                dma((2,)),
                dma((2,)),
            ],
            compiler_params=pltpu.CompilerParams(
                collective_id=0, has_side_effects=True, vmem_limit_bytes=60 * 1024 * 1024
            ),
        )(
            cell_type, groove_mask, dist,
            jnp.asarray(forward), jnp.asarray(inverse), jnp.asarray(height),
            jnp.asarray(tables), jnp.asarray(rows), jnp.asarray(lanes),
        )

    return jax.shard_map(
        local,
        mesh=mesh,
        in_specs=(P("sub", "vel", "groups"), P("groups"), P("groups")),
        out_specs=P("sub", "vel", "groups"),
        check_vma=False,
    )
```
